32 devices in a mesh: groups: 2 (over y), adapter: 4 (over z), tensor: 4 (over x, core).
Axes of the slice: x: 2, y: 2, z: 4, core: 2. Of those that a mesh axis runs over, the one named last changes fastest.
Arguments:
- normed_layer_inputs: bfloat16 [4, 512, 8192], P(None, ('groups', 'adapter'), 'tensor'), parts along dimension 1, may hold values from -6 to 6
- key_value_weight: bfloat16 [8192, 1024], P('tensor'), may hold values from -0.0625 to 0.0625
- adapter_down_weight: bfloat16 [8, 8192, 128], P(('groups', 'adapter'), 'tensor'), parts along dimension 0, may hold values from -0.0625 to 0.0625
- adapter_up_weight: bfloat16 [8, 2, 64, 512], P(('groups', 'adapter')), parts along dimension 0, may hold values from -0.75 to 0.75
- request_adapter_index: int32 [512, 1], P(('groups', 'adapter')), parts along dimension 0, may hold values from 0 to 3; in each aligned block of 64 rows (0 to 63, 64 to 127, ...) at most 48 rows name the same one
- queries: bfloat16 [4, 512, 4096], P(None, ('groups', 'adapter'), 'tensor'), parts along dimension 1, may hold values from -4.6 to 4.6
- stored_cache_keys: bfloat16 [512, 64, 512], P(('groups', 'adapter', 'tensor')), parts along dimension 0, may hold values from -4.6 to 4.6
- stored_cache_values: bfloat16 [512, 64, 512], P(('groups', 'adapter', 'tensor')), parts along dimension 0, may hold values from -6 to 6
- filled_cache_length: int32 [512], P(('groups', 'adapter', 'tensor')), parts along dimension 0, may hold values from 2 to 64
Outputs:
- context: bfloat16 [4, 512, 4096], P(None, ('groups', 'adapter'), 'tensor'), parts along dimension 1
- new_kv: bfloat16 [4, 512, 1024], P(None, ('groups', 'adapter', 'tensor')), parts along dimension 1
The draws below stay inside these ranges and needn't reach their ends.
There are 2 independent parts, one for each index of `groups`. The reference program is written for one: setup_inputs(seed, part) draws one part's arguments, and reference() takes and returns one part's arrays. A program takes and returns all parts, laid end to end along the dimension named above; an argument that names none is the same for every part. Nothing has to cross between parts.
Inputs may be any that keep to these rules, and one draw needn't show every extreme that they name: `request_adapter_index`: among the 64 requests of each index of the adapter axis no adapter is named more than 48 times, and exactly 48 times in some such block.
All inputs are finite; a program needn't handle non-finite values.
Results may differ from the reference program's by a relative error of at most 0.0057.
Values may be sent and summed in bfloat16 or wider, within the bound.
A program may use at most 64 MiB of HBM per device.

```python
import math
import jax
import jax.numpy as jnp
import numpy as np
from jax import lax

MODEL_WIDTH = 8192
HQ = 32
KV = 4
HD = 128
ADAPTER_RANK = 64
STEPS = 4
ROWS_DEV = 64
CACHE = 64
KEY_VALUE_WIDTH = 512
ROWS = 256
ADAPTER_COUNT = 4
CAP = 48


def draw_queries(key, part):
    key = jax.random.fold_in(key, 1)
    drawn = jnp.clip(jax.random.normal(key, (STEPS, ROWS, HQ * HD), jnp.float32), -4.6, 4.6)
    return drawn.astype(jnp.bfloat16)


def draw_stored_cache_keys(key, part):
    key = jax.random.fold_in(key, 2)
    drawn = jnp.clip(jax.random.normal(key, (ROWS, CACHE, KEY_VALUE_WIDTH), jnp.float32), -4.6, 4.6)
    return drawn.astype(jnp.bfloat16)


def draw_filled_cache_length(key, part):
    key = jax.random.fold_in(key, 3)
    lengths = jax.random.randint(key, (ROWS,), 2, CACHE + 1)
    longest = jax.random.randint(jax.random.fold_in(key, 4), (), 0, ROWS)
    return jnp.where(jnp.arange(ROWS) == longest, CACHE, lengths).astype(jnp.int32)


def levels(rng, shape, cuts, least, top_value):
    factor_of, own = 1.0, jax.random.fold_in(rng, 6)
    for dim, blocks in cuts:
        draws = jnp.exp(jax.random.uniform(jax.random.fold_in(own, dim), (blocks,), jnp.float32, least / len(cuts), top_value / len(cuts)))
        factor_of = factor_of * jnp.repeat(draws, shape[dim] // blocks).reshape([-1 if axis == dim else 1 for axis in range(len(shape))])
    return factor_of


def assign_block(rng, own, number, rows, count, top, most, skew):
    ranking = jax.random.permutation(rng, count)
    crowded, usual = shares(count, rows * top, most, skew, True), shares(count, rows * top, most, skew, False)
    places = jnp.arange(count)

    def named(tallies, rotation):
        used = int((tallies > 0).sum())
        fixed = max(1, used // 4)
        moved = fixed + (places - fixed + rotation * (used - fixed)) % max(1, count - fixed)
        return jnp.zeros((count,), jnp.int32).at[ranking[jnp.where(places < fixed, places, moved)]].set(jnp.asarray(tallies, jnp.int32))

    tallies = jnp.where(number % 4 == 0, named(crowded, number // 4), named(usual, number - number // 4 - 1))
    mixed = jax.random.permutation(jax.random.fold_in(own, 3), count)
    giver, receiver = mixed[0:count // 2 * 2:2], mixed[1:count // 2 * 2:2]
    room = jnp.minimum(tallies[giver] - 1, most - tallies[receiver]) // 2
    room = jnp.where((giver == ranking[0]) | (receiver == ranking[0]) | (tallies[receiver] == 0), 0, jnp.maximum(room, 0))
    moved = jax.random.randint(jax.random.fold_in(own, 4), (count // 2,), 0, 1 << 20) % (room + 1)
    tallies = tallies.at[giver].add(-moved).at[receiver].add(moved)
    labels = jnp.searchsorted(jnp.cumsum(tallies), jnp.arange(rows * top), side="right").astype(jnp.int32)
    grid = labels.reshape(top, rows).T
    grid = grid[jax.random.permutation(jax.random.fold_in(own, 1), rows)]
    rotation = jax.random.randint(jax.random.fold_in(own, 2), (rows, 1), 0, top)
    return jnp.take_along_axis(grid, (jnp.arange(top)[None, :] + rotation) % top, axis=1)


def shares(number_of, total, bound, skew, full):
    loads = [(1 << 20) // math.isqrt(grade ** skew) + 1 for grade in range(1, number_of + 1)]
    largest = bound if full else min(bound, max(-(-total // number_of), total * loads[0] // sum(loads)))
    least = 1 if total - largest >= number_of - 1 else 0
    counts, surplus = [largest] + [least] * (number_of - 1), total - largest - least * (number_of - 1)
    while surplus > 0:
        candidates = [i for i in range(1, number_of) if counts[i] < largest] or [i for i in range(1, number_of) if counts[i] < bound]
        pool, left = sum([loads[i] for i in candidates]), surplus
        for i in candidates:
            addition = min(bound - counts[i], max(1, left * loads[i] // pool), surplus)
            counts[i] = counts[i] + addition
            surplus = surplus - addition
    return np.array(counts)


def noise(stream_key, dims, scale, most, split=(), held_as=jnp.bfloat16):
    entries = jax.random.normal(stream_key, dims, jnp.float32) * scale
    if len(split) > 0:
        entries = levels(stream_key, dims, split, -0.22, 0.18) * entries
    return jnp.clip(entries, min=-most, max=most).astype(held_as)


def setup_inputs(seed: int = 0, part: int = 0) -> dict:
    seeds = jax.random.split(jax.random.key(seed), 10)
    part_splits = jax.random.split(jax.random.fold_in(seeds[9], part), 10)
    normed_layer_inputs = noise(part_splits[0], (STEPS, ROWS, MODEL_WIDTH), 1.0, 6.0, ((1, 4), (2, 4)))
    key_value_weight = noise(seeds[1], (MODEL_WIDTH, 2 * KEY_VALUE_WIDTH), MODEL_WIDTH ** -0.5, 0.0625, ((0, 4),))
    adapter_down_weight = noise(part_splits[2], (ADAPTER_COUNT, MODEL_WIDTH, 2 * ADAPTER_RANK), MODEL_WIDTH ** -0.5, 0.0625, ((0, 4), (1, 4)))
    adapter_up_weight = noise(part_splits[3], (ADAPTER_COUNT, 2, ADAPTER_RANK, KEY_VALUE_WIDTH), ADAPTER_RANK ** -0.5, 0.75, ((0, 4),))
    request_adapter_index_keys = jax.random.split(jax.random.fold_in(part_splits[4], 1), ROWS // ROWS_DEV)
    request_adapter_index_turns = jax.random.permutation(jax.random.fold_in(part_splits[4], 3), ROWS // ROWS_DEV)
    request_adapter_index = jax.vmap(lambda own, number: assign_block(jax.random.fold_in(part_splits[4], 2), own, number, ROWS_DEV, ADAPTER_COUNT, 1, CAP, 2))(request_adapter_index_keys, request_adapter_index_turns).reshape((ROWS, 1))
    queries = draw_queries(jax.random.fold_in(jax.random.fold_in(seeds[9], part), 71), part)
    stored_cache_keys = draw_stored_cache_keys(jax.random.fold_in(jax.random.fold_in(seeds[9], part), 71), part)
    stored_cache_values = noise(part_splits[7], (ROWS, CACHE, KEY_VALUE_WIDTH), 1.0, 6.0, ((0, 16),))
    filled_cache_length = draw_filled_cache_length(jax.random.fold_in(jax.random.fold_in(seeds[9], part), 71), part)
    return {"normed_layer_inputs": normed_layer_inputs, "key_value_weight": key_value_weight, "adapter_down_weight": adapter_down_weight, "adapter_up_weight": adapter_up_weight, "request_adapter_index": request_adapter_index, "queries": queries, "stored_cache_keys": stored_cache_keys, "stored_cache_values": stored_cache_values, "filled_cache_length": filled_cache_length}


def rotate_keys(key_rows, positions):
    shaped = key_rows.reshape(key_rows.shape[:-1] + (KV, HD))
    key_width = HD // 2
    pair_index = jnp.arange(key_width, dtype=jnp.float32)
    frequency = jnp.exp(-(2.0 * pair_index / HD) * math.log(500000.0))
    angles = positions[:, :, None, None] * frequency
    cosine = jnp.cos(angles)
    sine = jnp.sin(angles)
    first_half = shaped[..., :key_width]
    second_half = shaped[..., key_width:]
    turned = jnp.concatenate([first_half * cosine - second_half * sine, second_half * cosine + first_half * sine], -1)
    return turned.reshape(key_rows.shape)

def attend(queries, stored_cache_keys, stored_cache_values, filled_cache_length, new_kv):
    step_count, row_count = (queries.shape[0], queries.shape[1])
    cache_len = stored_cache_keys.shape[1]
    new_keys = jnp.swapaxes(new_kv[..., :KEY_VALUE_WIDTH], 0, 1)
    new_values = jnp.swapaxes(new_kv[..., KEY_VALUE_WIDTH:], 0, 1)
    all_keys = jnp.concatenate([stored_cache_keys, new_keys], 1)
    all_values = jnp.concatenate([stored_cache_values, new_values], 1)
    span = all_keys.shape[1]
    group_size = HQ // KV
    query_heads = queries.reshape(step_count, row_count, KV, group_size, HD).astype(jnp.float32)
    key_heads = all_keys.reshape(row_count, span, KV, HD).astype(jnp.float32)
    value_heads = all_values.reshape(row_count, span, KV, HD).astype(jnp.float32)
    scores = jnp.einsum('srkgd,rpkd->srkgp', query_heads, key_heads) * (1.0 / math.sqrt(HD))
    position = jnp.arange(span, dtype=jnp.int32)
    in_cache = position[None, None, :] < filled_cache_length[None, :, None]
    in_new = (position - cache_len)[None, None, :] <= jnp.arange(step_count, dtype=jnp.int32)[:, None, None]
    visible = jnp.where(position[None, None, :] < cache_len, in_cache, in_new)
    scores = jnp.where(visible[:, :, None, None, :], scores, jnp.float32(-1e+30))
    row_max = lax.optimization_barrier(jnp.max(scores, axis=-1, keepdims=True))
    exponent = jnp.exp(scores - row_max)
    totals = lax.optimization_barrier(jnp.sum(exponent, axis=-1, keepdims=True))
    weights = exponent.astype(jnp.bfloat16)
    context = jnp.einsum('srkgp,rpkd->srkgd', weights.astype(jnp.float32), value_heads) / totals
    return context.reshape(step_count, row_count, HQ * HD).astype(jnp.bfloat16)

def reference(normed_layer_inputs, key_value_weight, adapter_down_weight, adapter_up_weight, request_adapter_index, queries, stored_cache_keys, stored_cache_values, filled_cache_length):
    base = jnp.dot(normed_layer_inputs.reshape(STEPS * ROWS, MODEL_WIDTH), key_value_weight, preferred_element_type=jnp.float32).reshape(STEPS, ROWS, 2 * KEY_VALUE_WIDTH)
    adapter_of = request_adapter_index[:, 0]

    def one_request(item):
        per_request_rows, identity_matrix = item
        shrink_product = jnp.dot(per_request_rows, adapter_down_weight[identity_matrix], preferred_element_type=jnp.float32).astype(jnp.bfloat16)
        gathered_up_weight = adapter_up_weight[identity_matrix]
        key_projection_part = jnp.dot(shrink_product[:, :ADAPTER_RANK], gathered_up_weight[0], preferred_element_type=jnp.float32)
        value_projection_part = jnp.dot(shrink_product[:, ADAPTER_RANK:], gathered_up_weight[1], preferred_element_type=jnp.float32)
        return jnp.concatenate([key_projection_part, value_projection_part], -1).astype(jnp.bfloat16)
    delta = lax.map(one_request, (jnp.swapaxes(normed_layer_inputs, 0, 1), adapter_of))
    fresh = base + jnp.swapaxes(delta, 0, 1).astype(jnp.float32)
    positions = (filled_cache_length[None, :] + jnp.arange(STEPS, dtype=jnp.int32)[:, None]).astype(jnp.float32)
    turned = rotate_keys(fresh[..., :KEY_VALUE_WIDTH], positions)
    new_kv = jnp.concatenate([turned, fresh[..., KEY_VALUE_WIDTH:]], -1).astype(jnp.bfloat16)
    context = attend(queries, stored_cache_keys, stored_cache_values, filled_cache_length, new_kv)
    return (context, new_kv)
```

```python
import functools
import math

import jax
import jax.numpy as jnp
import numpy as np
from jax import lax
from jax.experimental import pallas as pl
from jax.experimental.pallas import tpu as pltpu
from jax.sharding import PartitionSpec as P

HQ = 32
KV = 4
HD = 128
KEY_VALUE_WIDTH = 512
GROUP = HQ // KV
MESH = pl.DeviceIdType.MESH
F32 = jnp.float32
BF16 = jnp.bfloat16


def kernel(
    n_a, n_t, chunks,
    idx_ref, cos_ref, sin_ref, colok_ref, same_ref, perm_ref,
    x_hbm, w_hbm, a_hbm, u_hbm, q_hbm, k_hbm, v_hbm,
    ctx_hbm, new_ref,
    x_ref, w_ref, down, up, k_ref, v_ref, q_all, qp,
    part, base_in, shr, shr_in, newp, ctxs,
    loc, a_send, a_recv, u_send, u_recv, uz_send, uz_recv,
    q_send, q_recv, b_send, b_recv, s_send, s_recv, c_send, c_recv,
):
    z = lax.axis_index("adapter")
    t = lax.axis_index("tensor")
    steps, rows, depth = x_ref.shape
    own = rows // n_t
    width = w_ref.shape[1]
    tile = steps * rows
    otile = steps * own
    cd = depth // chunks
    uq = up.shape[2]
    hl = q_hbm.shape[2]
    hpt = hl // HD

    x_cp = pltpu.make_async_copy(x_hbm, x_ref, loc.at[0])
    w_cp = pltpu.make_async_copy(w_hbm, w_ref, loc.at[1])
    a_cp = pltpu.make_async_copy(a_hbm.at[0], down.at[z], loc.at[2])
    u_cp = pltpu.make_async_copy(u_hbm.at[t], up.at[z, t], loc.at[3])
    q_cp = pltpu.make_async_copy(
        q_hbm.at[:, pl.ds(pl.multiple_of(t * own, own), own)], q_all.at[t], loc.at[4])
    k_cp = pltpu.make_async_copy(k_hbm, k_ref, loc.at[5])
    v_cp = pltpu.make_async_copy(v_hbm, v_ref, loc.at[6])
    for cp in (a_cp, u_cp, x_cp, w_cp, q_cp, k_cp, v_cp):
        cp.start()

    barrier = pltpu.get_barrier_semaphore()
    for d in range(1, n_t):
        pl.semaphore_signal(barrier, inc=1, device_id={"tensor": lax.rem(t + d, n_t)}, device_id_type=MESH)

    @pl.when(z > 0)
    def _():
        pl.semaphore_signal(barrier, inc=1, device_id={"adapter": z - 1}, device_id_type=MESH)

    @pl.when(z < n_a - 1)
    def _():
        pl.semaphore_signal(barrier, inc=1, device_id={"adapter": z + 1}, device_id_type=MESH)

    pl.semaphore_wait(barrier, n_t - 1 + jnp.where(z > 0, 1, 0) + jnp.where(z < n_a - 1, 1, 0))

    def a_copy(direction, k, c):
        a = z - k if direction == 0 else z + k
        to = z + 1 if direction == 0 else z - 1
        block = down.at[a, pl.ds(c * cd, cd)]
        return pltpu.make_async_remote_copy(
            src_ref=block, dst_ref=block, send_sem=a_send.at[direction, k, c],
            recv_sem=a_recv.at[direction, k, c], device_id={"adapter": to}, device_id_type=MESH)

    def uz_copy(direction, k):
        a = z - k if direction == 0 else z + k
        to = z + 1 if direction == 0 else z - 1
        block = up.at[a, t]
        return pltpu.make_async_remote_copy(
            src_ref=block, dst_ref=block, send_sem=uz_send.at[direction, k],
            recv_sem=uz_recv.at[direction, k], device_id={"adapter": to}, device_id_type=MESH)

    def held(direction, k):
        return z >= k if direction == 0 else z + k < n_a

    def sends(direction, k):
        return jnp.logical_and(held(direction, k), z < n_a - 1 if direction == 0 else z > 0)

    def u_copy(a, slot, d):
        block = up.at[a, t]
        return pltpu.make_async_remote_copy(
            src_ref=block, dst_ref=block, send_sem=u_send.at[slot, d - 1],
            recv_sem=u_recv.at[slot, d - 1], device_id={"tensor": lax.rem(t + d, n_t)}, device_id_type=MESH)

    def arrived_a(direction, k, c):
        a = z - k if direction == 0 else z + k
        block = down.at[a, pl.ds(c * cd, cd)]
        pltpu.make_async_copy(block, block, a_recv.at[direction, k - 1, c]).wait()

    def arrived_uz(direction, k):
        a = z - k if direction == 0 else z + k
        block = up.at[a, t]
        pltpu.make_async_copy(block, block, uz_recv.at[direction, k - 1]).wait()

    u_cp.wait()
    for direction in range(2):
        @pl.when(sends(direction, 0))
        def _(direction=direction):
            uz_copy(direction, 0).start()
    a_cp.wait()
    for c in range(chunks):
        for direction in range(2):
            @pl.when(sends(direction, 0))
            def _(direction=direction, c=c):
                a_copy(direction, 0, c).start()

    def q_copy(d):
        to = lax.rem(t + d, n_t)
        return pltpu.make_async_remote_copy(
            src_ref=q_hbm.at[:, pl.ds(pl.multiple_of(to * own, own), own)], dst_ref=q_all.at[t],
            send_sem=q_send.at[d - 1], recv_sem=q_recv.at[d - 1], device_id={"tensor": to}, device_id_type=MESH)

    def b_copy(d):
        to = lax.rem(t + d, n_t)
        return pltpu.make_async_remote_copy(
            src_ref=part.at[:, pl.ds(pl.multiple_of(to * own, own), own)], dst_ref=base_in.at[d - 1],
            send_sem=b_send.at[d - 1], recv_sem=b_recv.at[d - 1], device_id={"tensor": to}, device_id_type=MESH)

    def s_copy(d):
        to = lax.rem(t + d, n_t)
        return pltpu.make_async_remote_copy(
            src_ref=shr.at[:, pl.ds(pl.multiple_of(to * own, own), own)], dst_ref=shr_in.at[d - 1],
            send_sem=s_send.at[d - 1], recv_sem=s_recv.at[d - 1], device_id={"tensor": to}, device_id_type=MESH)

    for d in range(1, n_t):
        u_copy(z, 0, d).start()
        q_copy(d).start()

    x_cp.wait()
    w_cp.wait()
    bn = 256

    def base_step(i, carry):
        cols = pl.ds(pl.multiple_of(i * bn, bn), bn)
        part[:, :, cols] = jnp.dot(
            x_ref[...].reshape(tile, depth), w_ref[:, cols], preferred_element_type=F32
        ).reshape(steps, rows, bn)
        return carry

    lax.fori_loop(0, width // bn, base_step, 0)
    for d in range(1, n_t):
        b_copy(d).start()

    idx = jnp.concatenate([idx_ref[...]] * steps, axis=0)
    rank = down.shape[2]

    def shrink_part(a, lo, size):
        got = jnp.dot(
            x_ref[:, :, pl.ds(lo, size)].reshape(tile, size), down[a, pl.ds(lo, size)],
            preferred_element_type=F32)
        return jnp.where(idx == a, got, 0.0).reshape(steps, rows, rank)

    shr[...] = shrink_part(z, 0, depth)

    for k in range(1, n_a):
        for direction in range(2):
            @pl.when(held(direction, k))
            def _(direction=direction, k=k):
                arrived_uz(direction, k)
                a = z - k if direction == 0 else z + k
                for d in range(1, n_t):
                    u_copy(a, 2 * k - 1 + direction, d).start()

            @pl.when(sends(direction, k))
            def _(direction=direction, k=k):
                uz_copy(direction, k).start()
        for c in range(chunks):
            for direction in range(2):
                @pl.when(held(direction, k))
                def _(direction=direction, k=k, c=c):
                    arrived_a(direction, k, c)

                @pl.when(sends(direction, k))
                def _(direction=direction, k=k, c=c):
                    a_copy(direction, k, c).start()

            for direction in range(2):
                @pl.when(held(direction, k))
                def _(direction=direction, k=k, c=c):
                    a = z - k if direction == 0 else z + k
                    shr[...] += shrink_part(a, c * cd, cd)

        if k == n_a - 2 or n_a == 2:
            q_cp.wait()
            for d in range(1, n_t):
                q_copy(d).wait()
            for j in range(n_t):
                qp[j] = jnp.dot(
                    perm_ref[...], q_all[j].reshape(otile, hl), preferred_element_type=F32).astype(BF16)
            for d in range(1, n_t):
                b_copy(d).wait()
            mine = pl.ds(pl.multiple_of(t * own, own), own)
            total = part[:, mine]
            for d in range(1, n_t):
                total = total + base_in[d - 1]
            base_in[0] = total
            k_cp.wait()
            v_cp.wait()

    for d in range(1, n_t):
        s_copy(d).start()
    for d in range(1, n_t):
        u_copy(z, 0, d).wait()
    for k in range(1, n_a):
        for direction in range(2):
            @pl.when(held(direction, k))
            def _(direction=direction, k=k):
                a = z - k if direction == 0 else z + k
                for d in range(1, n_t):
                    u_copy(a, 2 * k - 1 + direction, d).wait()
    for d in range(1, n_t):
        s_copy(d).wait()
    mine = pl.ds(pl.multiple_of(t * own, own), own)
    total = shr[:, mine]
    for d in range(1, n_t):
        total = total + shr_in[d - 1]
    shrunk = total.reshape(otile, rank)
    both = jnp.concatenate([shrunk, shrunk], axis=0)
    line = lax.broadcasted_iota(jnp.int32, (2 * otile, rank), 0)
    lane = lax.broadcasted_iota(jnp.int32, (2 * otile, rank), 1)
    both = jnp.where((line < otile) == (lane < rank // 2), both, 0.0)
    idx_own = idx_ref[mine]
    idx_both = jnp.concatenate([idx_own] * (2 * steps), axis=0)
    delta = jnp.zeros((2 * otile, KEY_VALUE_WIDTH), F32)
    for a in range(n_a):
        delta = delta + jnp.dot(
            jnp.where(idx_both == a, both, 0.0).astype(BF16),
            up[a].reshape(rank, KEY_VALUE_WIDTH), preferred_element_type=F32)
    delta = delta.astype(BF16).astype(F32)
    fresh = base_in[0].reshape(otile, width)
    pieces = []
    for h in range(KV):
        one = fresh[:, h * HD:(h + 1) * HD] + delta[:otile, h * HD:(h + 1) * HD]
        pieces.append(one * cos_ref[...] + pltpu.roll(one, HD // 2, 1) * sin_ref[...])
    pieces.append(fresh[:, KEY_VALUE_WIDTH:] + delta[otile:])
    new_kv = jnp.concatenate(pieces, axis=1).astype(BF16)
    new_ref[...] = new_kv.reshape(steps, own, width)
    newp[...] = jnp.dot(perm_ref[...], new_kv, preferred_element_type=F32).astype(BF16)

    def c_copy(d):
        to = lax.rem(t + d, n_t)
        return pltpu.make_async_remote_copy(
            src_ref=ctxs.at[d], dst_ref=ctx_hbm.at[:, pl.ds(pl.multiple_of(t * own, own), own)],
            send_sem=c_send.at[d - 1], recv_sem=c_recv.at[d - 1], device_id={"tensor": to}, device_id_type=MESH)

    per = same_ref.shape[1] // (k_ref.shape[1] + steps)
    scale = 1.0 / math.sqrt(HD)
    order = [n_t // 2] + [d for d in range(1, n_t) if d != n_t // 2] + [0]
    for d in order:
        to = lax.rem(t + d, n_t)
        g = to * hpt // GROUP
        kl = pl.ds(pl.multiple_of(g * HD, HD), HD)
        vl = pl.ds(pl.multiple_of(KEY_VALUE_WIDTH + g * HD, HD), HD)
        tiles = []
        for b in range(own // per):
            r0, n0 = b * per, per * steps
            lines = pl.ds(b * n0, n0)
            qt = jnp.concatenate([qp[to, lines, h * HD:(h + 1) * HD] for h in range(hpt)], axis=0)
            keys = jnp.concatenate(
                [k_ref[pl.ds(r0, per), :, kl].reshape(per * k_ref.shape[1], HD), newp[lines, kl]], axis=0)
            vals = jnp.concatenate(
                [v_ref[pl.ds(r0, per), :, kl].reshape(per * v_ref.shape[1], HD), newp[lines, vl]], axis=0)
            sc = lax.dot_general(qt, keys, (((1,), (1,)), ((), ())), preferred_element_type=F32) * scale
            sc = jnp.where(same_ref[...] * colok_ref[pl.ds(b, 1), :] > 0, sc, -1e30)
            e = jnp.exp(sc - jnp.max(sc, axis=1, keepdims=True))
            tot = jnp.sum(e, axis=1, keepdims=True)
            o = (jnp.dot(e.astype(BF16), vals, preferred_element_type=F32) / tot).astype(BF16)
            tiles.append(jnp.concatenate([o[h * n0:(h + 1) * n0] for h in range(hpt)], axis=1))
        ctxp = jnp.concatenate(tiles, axis=0)
        ctxs[d] = lax.dot_general(
            perm_ref[...], ctxp, (((0,), (0,)), ((), ())), preferred_element_type=F32
        ).astype(BF16).reshape(steps, own, hl)
        if d:
            c_copy(d).start()
    own_cp = pltpu.make_async_copy(ctxs.at[0], ctx_hbm.at[:, mine], loc.at[7])
    own_cp.start()

    for k in range(n_a):
        for direction in range(2):
            @pl.when(sends(direction, k))
            def _(direction=direction, k=k):
                uz_copy(direction, k).wait_send()
                for c in range(chunks):
                    a_copy(direction, k, c).wait_send()
    own_cp.wait()
    for d in range(1, n_t):
        c_copy(d).wait()


def body(
    normed_layer_inputs, key_value_weight, adapter_down_weight, adapter_up_weight,
    request_adapter_index, queries, stored_cache_keys, stored_cache_values, filled_cache_length,
):
    n_a = lax.axis_size("adapter")
    n_t = lax.axis_size("tensor")
    steps, rows, depth = normed_layer_inputs.shape
    own = rows // n_t
    otile = steps * own
    width = key_value_weight.shape[1]
    rank = adapter_down_weight.shape[2]
    cache = stored_cache_keys.shape[1]
    hl = queries.shape[2]
    hpt = hl // HD
    per = 16 // steps
    chunks = 4
    uq = rank // n_t

    i = np.arange(otile)
    perm = np.zeros((otile, otile), np.float32)
    perm[i, (i % steps) * own + i // steps] = 1
    line = np.arange(hpt * per * steps) % (per * steps)
    col_r = np.concatenate([np.repeat(np.arange(per), cache), np.repeat(np.arange(per), steps)])
    col_s = np.concatenate([np.full(per * cache, -1), np.tile(np.arange(steps), per)])
    same = (line[:, None] // steps == col_r[None]) & (col_s[None] <= line[:, None] % steps)
    filled = (jnp.arange(cache, dtype=jnp.int32)[None] < filled_cache_length[:, None]).astype(F32)
    colok = jnp.concatenate(
        [filled.reshape(own // per, per * cache), jnp.ones((own // per, per * steps), F32)], axis=1)
    idx = jnp.broadcast_to(request_adapter_index, (rows, rank))
    positions = (
        filled_cache_length[None, :] + jnp.arange(steps, dtype=jnp.int32)[:, None]
    ).astype(F32).reshape(otile, 1)
    half = HD // 2
    pair = jnp.arange(HD, dtype=jnp.int32) % half
    frequency = jnp.exp(-(2.0 * pair.astype(F32) / HD) * math.log(500000.0))
    angles = positions * frequency[None]
    cosine = jnp.cos(angles)
    sine = jnp.where(jnp.arange(HD)[None] < half, -jnp.sin(angles), jnp.sin(angles))

    vm = pl.BlockSpec(memory_space=pltpu.VMEM)
    hbm = pl.BlockSpec(memory_space=pl.ANY)
    dma = pltpu.SemaphoreType.DMA
    context, new_kv = pl.pallas_call(
        functools.partial(kernel, n_a, n_t, chunks),
        out_shape=(
            jax.ShapeDtypeStruct((steps, rows, hl), BF16),
            jax.ShapeDtypeStruct((steps, own, width), BF16),
        ),
        in_specs=[vm] * 6 + [hbm] * 7,
        out_specs=(hbm, vm),
        scratch_shapes=[
            pltpu.VMEM((steps, rows, depth), BF16),
            pltpu.VMEM((depth, width), BF16),
            pltpu.VMEM((n_a, depth, rank), BF16),
            pltpu.VMEM((n_a, n_t, uq, KEY_VALUE_WIDTH), BF16),
            pltpu.VMEM(stored_cache_keys.shape, BF16),
            pltpu.VMEM(stored_cache_values.shape, BF16),
            pltpu.VMEM((n_t, steps, own, hl), BF16),
            pltpu.VMEM((n_t, otile, hl), BF16),
            pltpu.VMEM((steps, rows, width), F32),
            pltpu.VMEM((n_t - 1, steps, own, width), F32),
            pltpu.VMEM((steps, rows, rank), F32),
            pltpu.VMEM((n_t - 1, steps, own, rank), F32),
            pltpu.VMEM((otile, width), BF16),
            pltpu.VMEM((n_t, steps, own, hl), BF16),
            dma((8,)),
            dma((2, n_a, chunks)), dma((2, n_a, chunks)),
            dma((2 * n_a, n_t - 1)), dma((2 * n_a, n_t - 1)),
            dma((2, n_a)), dma((2, n_a)),
            dma((n_t - 1,)), dma((n_t - 1,)),
            dma((n_t - 1,)), dma((n_t - 1,)),
            dma((n_t - 1,)), dma((n_t - 1,)),
            dma((n_t - 1,)), dma((n_t - 1,)),
        ],
        compiler_params=pltpu.CompilerParams(
            collective_id=0, has_side_effects=True, vmem_limit_bytes=48 * 1024 * 1024),
    )(
        idx, cosine, sine, colok, jnp.asarray(same, F32), jnp.asarray(perm, BF16),
        normed_layer_inputs, key_value_weight, adapter_down_weight,
        adapter_up_weight.reshape(n_t, uq, KEY_VALUE_WIDTH), queries,
        stored_cache_keys, stored_cache_values,
    )
    return (context, new_kv)


def solution(mesh):
    in_specs = (
        P(None, ("groups", "adapter"), "tensor"),
        P("tensor", None),
        P(("groups", "adapter"), "tensor", None),
        P(("groups", "adapter"), None, None, None),
        P(("groups", "adapter"), None),
        P(None, ("groups", "adapter"), "tensor"),
        P(("groups", "adapter", "tensor"), None, None),
        P(("groups", "adapter", "tensor"), None, None),
        P(("groups", "adapter", "tensor")),
    )
    out_specs = (
        P(None, ("groups", "adapter"), "tensor"),
        P(None, ("groups", "adapter", "tensor"), None),
    )
    return jax.shard_map(body, mesh=mesh, in_specs=in_specs, out_specs=out_specs, check_vma=False)
```

```python
import functools
import math

import jax
import jax.numpy as jnp
from jax import lax
from jax.experimental import pallas as pl
from jax.experimental.pallas import tpu as pltpu
from jax.sharding import PartitionSpec as P

HQ = 32
KV = 4
HD = 128
KEY_VALUE_WIDTH = 512
GROUP = HQ // KV
MESH = pl.DeviceIdType.MESH
F32 = jnp.float32
BF16 = jnp.bfloat16


def kernel(
    n_a, n_t, chunks,
    idx_ref, len_ref,
    x_hbm, w_hbm, a_hbm, u_hbm, q_hbm, k_hbm, v_hbm,
    ctx_hbm, new_ref,
    x_ref, w_ref, down, up, k_ref, v_ref, q_all, qp,
    part, base_in, shr, shr_in, newp, ctxs, oc, mc, lc, idxs,
    loc, a_send, a_recv, u_send, u_recv, uz_send, uz_recv,
    q_send, q_recv, b_send, b_recv, s_send, s_recv, c_send, c_recv,
):
    z = lax.axis_index("adapter")
    t = lax.axis_index("tensor")
    steps, rows, depth = x_ref.shape
    own = rows // n_t
    width = w_ref.shape[1]
    tile = steps * rows
    otile = steps * own
    cd = depth // chunks
    uq = up.shape[2]
    hl = q_hbm.shape[2]
    hpt = hl // HD

    cache = k_ref.shape[1]
    per = 16 // steps
    n0 = per * steps
    tr = n0 * hpt
    iota = lax.broadcasted_iota
    I32 = jnp.int32
    scale = 1.0 / math.sqrt(HD)

    def column(row):
        n = row.shape[1]
        eye = iota(I32, (n, n), 0) == iota(I32, (n, n), 1)
        return jnp.sum(jnp.where(eye, row.astype(F32), 0.0), axis=1, keepdims=True)

    x_cp = pltpu.make_async_copy(x_hbm, x_ref, loc.at[0])
    w_cp = pltpu.make_async_copy(w_hbm, w_ref, loc.at[1])
    a_cp = pltpu.make_async_copy(a_hbm.at[0], down.at[z], loc.at[2])
    u_cp = pltpu.make_async_copy(u_hbm.at[t], up.at[z, t], loc.at[3])
    q_cp = pltpu.make_async_copy(
        q_hbm.at[:, pl.ds(pl.multiple_of(t * own, own), own)], q_all.at[t], loc.at[4])
    k_cp = pltpu.make_async_copy(k_hbm, k_ref, loc.at[5])
    v_cp = pltpu.make_async_copy(v_hbm, v_ref, loc.at[6])
    for cp in (a_cp, u_cp, x_cp, w_cp, q_cp, k_cp, v_cp):
        cp.start()

    barrier = pltpu.get_barrier_semaphore()
    for d in range(1, n_t):
        pl.semaphore_signal(barrier, inc=1, device_id={"tensor": lax.rem(t + d, n_t)}, device_id_type=MESH)

    @pl.when(z > 0)
    def _():
        pl.semaphore_signal(barrier, inc=1, device_id={"adapter": z - 1}, device_id_type=MESH)

    @pl.when(z < n_a - 1)
    def _():
        pl.semaphore_signal(barrier, inc=1, device_id={"adapter": z + 1}, device_id_type=MESH)

    pl.semaphore_wait(barrier, n_t - 1 + jnp.where(z > 0, 1, 0) + jnp.where(z < n_a - 1, 1, 0))

    def a_copy(direction, k, c):
        a = z - k if direction == 0 else z + k
        to = z + 1 if direction == 0 else z - 1
        block = down.at[a, pl.ds(c * cd, cd)]
        return pltpu.make_async_remote_copy(
            src_ref=block, dst_ref=block, send_sem=a_send.at[direction, k, c],
            recv_sem=a_recv.at[direction, k, c], device_id={"adapter": to}, device_id_type=MESH)

    def uz_copy(direction, k):
        a = z - k if direction == 0 else z + k
        to = z + 1 if direction == 0 else z - 1
        block = up.at[a, t]
        return pltpu.make_async_remote_copy(
            src_ref=block, dst_ref=block, send_sem=uz_send.at[direction, k],
            recv_sem=uz_recv.at[direction, k], device_id={"adapter": to}, device_id_type=MESH)

    def held(direction, k):
        return z >= k if direction == 0 else z + k < n_a

    def sends(direction, k):
        return jnp.logical_and(held(direction, k), z < n_a - 1 if direction == 0 else z > 0)

    def u_copy(a, slot, d):
        block = up.at[a, t]
        return pltpu.make_async_remote_copy(
            src_ref=block, dst_ref=block, send_sem=u_send.at[slot, d - 1],
            recv_sem=u_recv.at[slot, d - 1], device_id={"tensor": lax.rem(t + d, n_t)}, device_id_type=MESH)

    def arrived_a(direction, k, c):
        a = z - k if direction == 0 else z + k
        block = down.at[a, pl.ds(c * cd, cd)]
        pltpu.make_async_copy(block, block, a_recv.at[direction, k - 1, c]).wait()

    def arrived_uz(direction, k):
        a = z - k if direction == 0 else z + k
        block = up.at[a, t]
        pltpu.make_async_copy(block, block, uz_recv.at[direction, k - 1]).wait()

    u_cp.wait()
    for direction in range(2):
        @pl.when(sends(direction, 0))
        def _(direction=direction):
            uz_copy(direction, 0).start()
    a_cp.wait()
    for c in range(chunks):
        for direction in range(2):
            @pl.when(sends(direction, 0))
            def _(direction=direction, c=c):
                a_copy(direction, 0, c).start()

    def q_copy(d):
        to = lax.rem(t + d, n_t)
        return pltpu.make_async_remote_copy(
            src_ref=q_hbm.at[:, pl.ds(pl.multiple_of(to * own, own), own)], dst_ref=q_all.at[t],
            send_sem=q_send.at[d - 1], recv_sem=q_recv.at[d - 1], device_id={"tensor": to}, device_id_type=MESH)

    def b_copy(d):
        to = lax.rem(t + d, n_t)
        return pltpu.make_async_remote_copy(
            src_ref=part.at[:, pl.ds(pl.multiple_of(to * own, own), own)], dst_ref=base_in.at[d - 1],
            send_sem=b_send.at[d - 1], recv_sem=b_recv.at[d - 1], device_id={"tensor": to}, device_id_type=MESH)

    def s_copy(d):
        to = lax.rem(t + d, n_t)
        return pltpu.make_async_remote_copy(
            src_ref=shr.at[:, pl.ds(pl.multiple_of(to * own, own), own)], dst_ref=shr_in.at[d - 1],
            send_sem=s_send.at[d - 1], recv_sem=s_recv.at[d - 1], device_id={"tensor": to}, device_id_type=MESH)

    for d in range(1, n_t):
        u_copy(z, 0, d).start()
        q_copy(d).start()

    x_cp.wait()
    w_cp.wait()
    bn = 256

    def base_step(i, carry):
        cols = pl.ds(pl.multiple_of(i * bn, bn), bn)
        part[:, :, cols] = jnp.dot(
            x_ref[...].reshape(tile, depth), w_ref[:, cols], preferred_element_type=F32
        ).reshape(steps, rows, bn)
        return carry

    lax.fori_loop(0, width // bn, base_step, 0)
    for d in range(1, n_t):
        b_copy(d).start()

    rank = down.shape[2]
    idxs[...] = jnp.broadcast_to(column(idx_ref[...]).astype(I32), (rows, rank))
    idx = jnp.concatenate([idxs[...]] * steps, axis=0)
    i0 = iota(I32, (otile, otile), 0)
    perm = jnp.where(
        iota(I32, (otile, otile), 1) == (i0 % steps) * own + i0 // steps, 1.0, 0.0).astype(BF16)
    lens = jnp.concatenate([column(len_ref[...])] * steps, axis=0)
    lens_rs = jnp.dot(
        perm, jnp.broadcast_to(lens, (otile, HD)).astype(BF16), preferred_element_type=F32).astype(I32)
    pair = (iota(I32, (1, HD), 1) % (HD // 2)).astype(F32)
    frequency = jnp.exp(-(2.0 * pair / HD) * math.log(500000.0))
    angles = (lens + (iota(I32, (otile, 1), 0) // own).astype(F32)) * frequency
    cosine = jnp.cos(angles)
    sine = jnp.sin(angles)
    sine = jnp.where(iota(I32, (otile, HD), 1) < HD // 2, -sine, sine)
    row_of = iota(I32, (tr, per * cache), 0) % n0 // steps
    col_at = iota(I32, (tr, per * cache), 1)
    same_row = row_of == col_at // cache
    col_p = col_at % cache
    line2 = iota(I32, (tr, n0), 0) % n0
    col2 = iota(I32, (tr, n0), 1)
    same_new = (line2 // steps == col2 // steps) & (col2 % steps <= line2 % steps)

    order = [n_t // 2] + [d for d in range(1, n_t) if d != n_t // 2] + [0]

    def query_tile(to, lines):
        return jnp.concatenate([qp[to, lines, h * HD:(h + 1) * HD] for h in range(hpt)], axis=0)

    def over_cache(d):
        to = lax.rem(t + d, n_t)
        kl = pl.ds(pl.multiple_of(to * hpt // GROUP * HD, HD), HD)
        for b in range(own // per):
            keys = k_ref[pl.ds(b * per, per), :, kl].reshape(per * cache, HD)
            vals = v_ref[pl.ds(b * per, per), :, kl].reshape(per * cache, HD)
            sc = lax.dot_general(
                query_tile(to, pl.ds(b * n0, n0)), keys, (((1,), (1,)), ((), ())),
                preferred_element_type=F32) * scale
            limit = jnp.concatenate([lens_rs[b * n0:(b + 1) * n0, :1]] * hpt, axis=0)
            sc = jnp.where(same_row & (col_p < limit), sc, -1e30)
            top = jnp.max(sc, axis=1, keepdims=True)
            e = jnp.exp(sc - top)
            at = d * (own // per) + b
            mc[at] = jnp.broadcast_to(top, (tr, HD))
            lc[at] = jnp.broadcast_to(jnp.sum(e, axis=1, keepdims=True), (tr, HD))
            oc[at] = jnp.dot(e.astype(BF16), vals, preferred_element_type=F32)

    def shrink_part(a, lo, size):
        got = jnp.dot(
            x_ref[:, :, pl.ds(lo, size)].reshape(tile, size), down[a, pl.ds(lo, size)],
            preferred_element_type=F32)
        return jnp.where(idx == a, got, 0.0).reshape(steps, rows, rank)

    shr[...] = shrink_part(z, 0, depth)

    for k in range(1, n_a):
        if k == n_a - 1:
            q_cp.wait()
            for d in range(1, n_t):
                q_copy(d).wait()
            for j in range(n_t):
                qp[j] = jnp.dot(
                    perm, q_all[j].reshape(otile, hl), preferred_element_type=F32).astype(BF16)
            for d in range(1, n_t):
                b_copy(d).wait()
            mine = pl.ds(pl.multiple_of(t * own, own), own)
            total = part[:, mine]
            for d in range(1, n_t):
                total = total + base_in[d - 1]
            base_in[0] = total
            k_cp.wait()
            v_cp.wait()

        for direction in range(2):
            @pl.when(held(direction, k))
            def _(direction=direction, k=k):
                arrived_uz(direction, k)
                a = z - k if direction == 0 else z + k
                for d in range(1, n_t):
                    u_copy(a, 2 * k - 1 + direction, d).start()

            @pl.when(sends(direction, k))
            def _(direction=direction, k=k):
                uz_copy(direction, k).start()
        for c in range(chunks):
            if k == n_a - 1:
                for d in order[c::chunks]:
                    over_cache(d)
            for direction in range(2):
                @pl.when(held(direction, k))
                def _(direction=direction, k=k, c=c):
                    arrived_a(direction, k, c)

                @pl.when(sends(direction, k))
                def _(direction=direction, k=k, c=c):
                    a_copy(direction, k, c).start()

            for direction in range(2):
                @pl.when(held(direction, k))
                def _(direction=direction, k=k, c=c):
                    a = z - k if direction == 0 else z + k
                    shr[...] += shrink_part(a, c * cd, cd)

    for d in range(1, n_t):
        s_copy(d).start()
    for d in range(1, n_t):
        u_copy(z, 0, d).wait()
    for k in range(1, n_a):
        for direction in range(2):
            @pl.when(held(direction, k))
            def _(direction=direction, k=k):
                a = z - k if direction == 0 else z + k
                for d in range(1, n_t):
                    u_copy(a, 2 * k - 1 + direction, d).wait()
    for d in range(1, n_t):
        s_copy(d).wait()
    mine = pl.ds(pl.multiple_of(t * own, own), own)
    total = shr[:, mine]
    for d in range(1, n_t):
        total = total + shr_in[d - 1]
    shrunk = total.reshape(otile, rank)
    both = jnp.concatenate([shrunk, shrunk], axis=0)
    line = iota(I32, (2 * otile, rank), 0)
    lane = iota(I32, (2 * otile, rank), 1)
    both = jnp.where((line < otile) == (lane < rank // 2), both, 0.0)
    idx_own = idxs[mine]
    idx_both = jnp.concatenate([idx_own] * (2 * steps), axis=0)
    delta = jnp.zeros((2 * otile, KEY_VALUE_WIDTH), F32)
    for a in range(n_a):
        delta = delta + jnp.dot(
            jnp.where(idx_both == a, both, 0.0).astype(BF16),
            up[a].reshape(rank, KEY_VALUE_WIDTH), preferred_element_type=F32)
    delta = delta.astype(BF16).astype(F32)
    fresh = base_in[0].reshape(otile, width)
    pieces = []
    for h in range(KV):
        one = fresh[:, h * HD:(h + 1) * HD] + delta[:otile, h * HD:(h + 1) * HD]
        pieces.append(one * cosine + pltpu.roll(one, HD // 2, 1) * sine)
    pieces.append(fresh[:, KEY_VALUE_WIDTH:] + delta[otile:])
    new_kv = jnp.concatenate(pieces, axis=1).astype(BF16)
    new_ref[...] = new_kv.reshape(steps, own, width)
    newp[...] = jnp.dot(perm, new_kv, preferred_element_type=F32).astype(BF16)

    def c_copy(d):
        to = lax.rem(t + d, n_t)
        return pltpu.make_async_remote_copy(
            src_ref=ctxs.at[d], dst_ref=ctx_hbm.at[:, pl.ds(pl.multiple_of(t * own, own), own)],
            send_sem=c_send.at[d - 1], recv_sem=c_recv.at[d - 1], device_id={"tensor": to}, device_id_type=MESH)

    for d in order:
        to = lax.rem(t + d, n_t)
        g = to * hpt // GROUP
        kl = pl.ds(pl.multiple_of(g * HD, HD), HD)
        vl = pl.ds(pl.multiple_of(KEY_VALUE_WIDTH + g * HD, HD), HD)
        tiles = []
        for b in range(own // per):
            lines = pl.ds(b * n0, n0)
            at = d * (own // per) + b
            sc = lax.dot_general(
                query_tile(to, lines), newp[lines, kl], (((1,), (1,)), ((), ())),
                preferred_element_type=F32) * scale
            sc = jnp.where(same_new, sc, -1e30)
            top = jnp.maximum(mc[at], jnp.max(sc, axis=1, keepdims=True))
            e = jnp.exp(sc - top[:, :n0])
            less = jnp.exp(mc[at] - top)
            tot = lc[at] * less + jnp.sum(e, axis=1, keepdims=True)
            o = oc[at] * less + jnp.dot(e.astype(BF16), newp[lines, vl], preferred_element_type=F32)
            o = (o / tot).astype(BF16)
            tiles.append(jnp.concatenate([o[h * n0:(h + 1) * n0] for h in range(hpt)], axis=1))
        ctxp = jnp.concatenate(tiles, axis=0)
        ctxs[d] = lax.dot_general(
            perm, ctxp, (((0,), (0,)), ((), ())), preferred_element_type=F32
        ).astype(BF16).reshape(steps, own, hl)
        if d:
            c_copy(d).start()
    own_cp = pltpu.make_async_copy(ctxs.at[0], ctx_hbm.at[:, mine], loc.at[7])
    own_cp.start()

    for k in range(n_a):
        for direction in range(2):
            @pl.when(sends(direction, k))
            def _(direction=direction, k=k):
                uz_copy(direction, k).wait_send()
                for c in range(chunks):
                    a_copy(direction, k, c).wait_send()
    own_cp.wait()
    for d in range(1, n_t):
        c_copy(d).wait()


def body(
    normed_layer_inputs, key_value_weight, adapter_down_weight, adapter_up_weight,
    request_adapter_index, queries, stored_cache_keys, stored_cache_values, filled_cache_length,
):
    n_a = lax.axis_size("adapter")
    n_t = lax.axis_size("tensor")
    steps, rows, depth = normed_layer_inputs.shape
    own = rows // n_t
    otile = steps * own
    width = key_value_weight.shape[1]
    rank = adapter_down_weight.shape[2]
    hl = queries.shape[2]
    hpt = hl // HD
    per = 16 // steps
    chunks = 4
    uq = rank // n_t

    vm = pl.BlockSpec(memory_space=pltpu.VMEM)
    hbm = pl.BlockSpec(memory_space=pltpu.HBM)
    dma = pltpu.SemaphoreType.DMA
    context, new_kv = pl.pallas_call(
        functools.partial(kernel, n_a, n_t, chunks),
        out_shape=(
            jax.ShapeDtypeStruct((steps, rows, hl), BF16),
            jax.ShapeDtypeStruct((steps, own, width), BF16),
        ),
        in_specs=[vm] * 2 + [hbm] * 7,
        out_specs=(hbm, vm),
        scratch_shapes=[
            pltpu.VMEM((steps, rows, depth), BF16),
            pltpu.VMEM((depth, width), BF16),
            pltpu.VMEM((n_a, depth, rank), BF16),
            pltpu.VMEM((n_a, n_t, uq, KEY_VALUE_WIDTH), BF16),
            pltpu.VMEM(stored_cache_keys.shape, BF16),
            pltpu.VMEM(stored_cache_values.shape, BF16),
            pltpu.VMEM((n_t, steps, own, hl), BF16),
            pltpu.VMEM((n_t, otile, hl), BF16),
            pltpu.VMEM((steps, rows, width), F32),
            pltpu.VMEM((n_t - 1, steps, own, width), F32),
            pltpu.VMEM((steps, rows, rank), F32),
            pltpu.VMEM((n_t - 1, steps, own, rank), F32),
            pltpu.VMEM((otile, width), BF16),
            pltpu.VMEM((n_t, steps, own, hl), BF16),
            *[pltpu.VMEM((n_t * (own // per), hpt * per * steps, HD), F32)] * 3,
            pltpu.VMEM((rows, rank), jnp.int32),
            dma((8,)),
            dma((2, n_a, chunks)), dma((2, n_a, chunks)),
            dma((2 * n_a, n_t - 1)), dma((2 * n_a, n_t - 1)),
            dma((2, n_a)), dma((2, n_a)),
            dma((n_t - 1,)), dma((n_t - 1,)),
            dma((n_t - 1,)), dma((n_t - 1,)),
            dma((n_t - 1,)), dma((n_t - 1,)),
            dma((n_t - 1,)), dma((n_t - 1,)),
        ],
        compiler_params=pltpu.CompilerParams(
            collective_id=0, has_side_effects=True, vmem_limit_bytes=63 * 1024 * 1024),
    )(
        request_adapter_index.reshape(1, rows), filled_cache_length.reshape(1, own),
        normed_layer_inputs, key_value_weight, adapter_down_weight,
        adapter_up_weight.reshape(n_t, uq, KEY_VALUE_WIDTH), queries,
        stored_cache_keys, stored_cache_values,
    )
    return (context, new_kv)


def solution(mesh):
    in_specs = (
        P(None, ("groups", "adapter"), "tensor"),
        P("tensor", None),
        P(("groups", "adapter"), "tensor", None),
        P(("groups", "adapter"), None, None, None),
        P(("groups", "adapter"), None),
        P(None, ("groups", "adapter"), "tensor"),
        P(("groups", "adapter", "tensor"), None, None),
        P(("groups", "adapter", "tensor"), None, None),
        P(("groups", "adapter", "tensor")),
    )
    out_specs = (
        P(None, ("groups", "adapter"), "tensor"),
        P(None, ("groups", "adapter", "tensor"), None),
    )
    return jax.shard_map(body, mesh=mesh, in_specs=in_specs, out_specs=out_specs, check_vma=False)
```

```python
import functools
import math

import jax
import jax.numpy as jnp
from jax import lax
from jax.experimental import pallas as pl
from jax.experimental.pallas import tpu as pltpu
from jax.sharding import PartitionSpec as P

HQ = 32
KV = 4
HD = 128
KEY_VALUE_WIDTH = 512
GROUP = HQ // KV
MESH = pl.DeviceIdType.MESH
F32 = jnp.float32
BF16 = jnp.bfloat16


def kernel(
    n_a, n_t, chunks,
    idx_ref, len_ref,
    x_hbm, w_hbm, a_hbm, u_hbm, q_hbm, k_hbm, v_hbm,
    ctx_hbm, new_ref,
    x_ref, w_ref, down, up, k_ref, v_ref, q_all, qp,
    part, base_in, shr, shr_in, newp, ctxs, oc, mc, lc, idxs, gx, gidx, gshr, gshr_in,
    guest, loc, a_send, a_recv, u_send, u_recv, uz_send, uz_recv,
    q_send, q_recv, b_send, b_recv, s_send, s_recv, c_send, c_recv,
):
    z = lax.axis_index("adapter")
    t = lax.axis_index("tensor")
    steps, rows, depth = x_ref.shape
    own = rows // n_t
    width = w_ref.shape[1]
    tile = steps * rows
    otile = steps * own
    cd = depth // chunks
    uq = up.shape[2]
    hl = q_hbm.shape[2]
    hpt = hl // HD

    cache = k_ref.shape[1]
    per = 16 // steps
    n0 = per * steps
    tr = n0 * hpt
    iota = lax.broadcasted_iota
    I32 = jnp.int32
    scale = 1.0 / math.sqrt(HD)

    def column(row):
        n = row.shape[1]
        eye = iota(I32, (n, n), 0) == iota(I32, (n, n), 1)
        return jnp.sum(jnp.where(eye, row.astype(F32), 0.0), axis=1, keepdims=True)

    x_cp = pltpu.make_async_copy(x_hbm, x_ref, loc.at[0])
    w_cp = pltpu.make_async_copy(w_hbm, w_ref, loc.at[1])
    a_cp = pltpu.make_async_copy(a_hbm.at[0], down.at[z], loc.at[2])
    u_cp = pltpu.make_async_copy(u_hbm.at[t], up.at[z, t], loc.at[3])
    q_cp = pltpu.make_async_copy(
        q_hbm.at[:, pl.ds(pl.multiple_of(t * own, own), own)], q_all.at[t], loc.at[4])
    k_cp = pltpu.make_async_copy(k_hbm, k_ref, loc.at[5])
    v_cp = pltpu.make_async_copy(v_hbm, v_ref, loc.at[6])
    for cp in (a_cp, u_cp, x_cp, w_cp, q_cp, k_cp, v_cp):
        cp.start()

    rank = down.shape[2]
    idxs[...] = jnp.broadcast_to(column(idx_ref[...]).astype(I32), (rows, rank))

    gc = 3 if n_a >= 4 else 0
    gs = gc * cd
    is_end = jnp.logical_or(z == 0, z == n_a - 1)
    is_host = jnp.logical_or(z == 1, z == n_a - 2)
    host_of = jnp.where(z == 0, 1, n_a - 2)
    end_of = jnp.where(z == 1, 0, n_a - 1)

    def guest_copy(i, src, dst, to):
        return pltpu.make_async_remote_copy(
            src_ref=src, dst_ref=dst, send_sem=guest.at[2 * i], recv_sem=guest.at[2 * i + 1],
            device_id={"adapter": to}, device_id_type=MESH)

    def gx_copy():
        return guest_copy(0, x_hbm.at[:, :, pl.ds(0, gs)], gx, host_of)

    def gi_copy():
        return guest_copy(1, idxs, gidx, host_of)

    def gr_copy():
        return guest_copy(2, gshr, gshr_in, end_of)

    barrier = pltpu.get_barrier_semaphore()
    for d in range(1, n_t):
        pl.semaphore_signal(barrier, inc=1, device_id={"tensor": lax.rem(t + d, n_t)}, device_id_type=MESH)

    @pl.when(z > 0)
    def _():
        pl.semaphore_signal(barrier, inc=1, device_id={"adapter": z - 1}, device_id_type=MESH)

    @pl.when(z < n_a - 1)
    def _():
        pl.semaphore_signal(barrier, inc=1, device_id={"adapter": z + 1}, device_id_type=MESH)

    pl.semaphore_wait(barrier, n_t - 1 + jnp.where(z > 0, 1, 0) + jnp.where(z < n_a - 1, 1, 0))

    def a_copy(direction, k, c):
        a = z - k if direction == 0 else z + k
        to = z + 1 if direction == 0 else z - 1
        block = down.at[a, pl.ds(c * cd, cd)]
        return pltpu.make_async_remote_copy(
            src_ref=block, dst_ref=block, send_sem=a_send.at[direction, k, c],
            recv_sem=a_recv.at[direction, k, c], device_id={"adapter": to}, device_id_type=MESH)

    def uz_copy(direction, k):
        a = z - k if direction == 0 else z + k
        to = z + 1 if direction == 0 else z - 1
        block = up.at[a, t]
        return pltpu.make_async_remote_copy(
            src_ref=block, dst_ref=block, send_sem=uz_send.at[direction, k],
            recv_sem=uz_recv.at[direction, k], device_id={"adapter": to}, device_id_type=MESH)

    def held(direction, k):
        return z >= k if direction == 0 else z + k < n_a

    def sends(direction, k):
        return jnp.logical_and(held(direction, k), z < n_a - 1 if direction == 0 else z > 0)

    def arrives(direction, k, c):
        if c >= gc:
            return held(direction, k)
        return jnp.logical_and(held(direction, k), z < n_a - 1 if direction == 0 else z > 0)

    def a_sends(direction, k, c):
        if c >= gc:
            return sends(direction, k)
        return jnp.logical_and(held(direction, k), z < n_a - 2 if direction == 0 else z > 1)

    def u_copy(a, slot, d):
        block = up.at[a, t]
        return pltpu.make_async_remote_copy(
            src_ref=block, dst_ref=block, send_sem=u_send.at[slot, d - 1],
            recv_sem=u_recv.at[slot, d - 1], device_id={"tensor": lax.rem(t + d, n_t)}, device_id_type=MESH)

    def arrived_a(direction, k, c):
        a = z - k if direction == 0 else z + k
        block = down.at[a, pl.ds(c * cd, cd)]
        pltpu.make_async_copy(block, block, a_recv.at[direction, k - 1, c]).wait()

    def arrived_uz(direction, k):
        a = z - k if direction == 0 else z + k
        block = up.at[a, t]
        pltpu.make_async_copy(block, block, uz_recv.at[direction, k - 1]).wait()

    u_cp.wait()
    for direction in range(2):
        @pl.when(sends(direction, 0))
        def _(direction=direction):
            uz_copy(direction, 0).start()
    a_cp.wait()
    for c in range(chunks):
        for direction in range(2):
            @pl.when(a_sends(direction, 0, c))
            def _(direction=direction, c=c):
                a_copy(direction, 0, c).start()

        if gc and c == chunks // 2 - 1:
            @pl.when(is_end)
            def _():
                gi_copy().start()
                gx_copy().start()

    def q_copy(d):
        to = lax.rem(t + d, n_t)
        return pltpu.make_async_remote_copy(
            src_ref=q_hbm.at[:, pl.ds(pl.multiple_of(to * own, own), own)], dst_ref=q_all.at[t],
            send_sem=q_send.at[d - 1], recv_sem=q_recv.at[d - 1], device_id={"tensor": to}, device_id_type=MESH)

    def b_copy(d):
        to = lax.rem(t + d, n_t)
        return pltpu.make_async_remote_copy(
            src_ref=part.at[:, pl.ds(pl.multiple_of(to * own, own), own)], dst_ref=base_in.at[d - 1],
            send_sem=b_send.at[d - 1], recv_sem=b_recv.at[d - 1], device_id={"tensor": to}, device_id_type=MESH)

    def s_copy(d):
        to = lax.rem(t + d, n_t)
        return pltpu.make_async_remote_copy(
            src_ref=shr.at[:, pl.ds(pl.multiple_of(to * own, own), own)], dst_ref=shr_in.at[d - 1],
            send_sem=s_send.at[d - 1], recv_sem=s_recv.at[d - 1], device_id={"tensor": to}, device_id_type=MESH)

    for d in range(1, n_t):
        u_copy(z, 0, d).start()
        q_copy(d).start()

    x_cp.wait()
    w_cp.wait()
    bn = 256

    def base_step(i, carry):
        cols = pl.ds(pl.multiple_of(i * bn, bn), bn)
        part[:, :, cols] = jnp.dot(
            x_ref[...].reshape(tile, depth), w_ref[:, cols], preferred_element_type=F32
        ).reshape(steps, rows, bn)
        return carry

    lax.fori_loop(0, width // bn, base_step, 0)
    for d in range(1, n_t):
        b_copy(d).start()

    idx = jnp.concatenate([idxs[...]] * steps, axis=0)
    i0 = iota(I32, (otile, otile), 0)
    perm = jnp.where(
        iota(I32, (otile, otile), 1) == (i0 % steps) * own + i0 // steps, 1.0, 0.0).astype(BF16)
    lens = jnp.concatenate([column(len_ref[...])] * steps, axis=0)
    lens_rs = jnp.dot(
        perm, jnp.broadcast_to(lens, (otile, HD)).astype(BF16), preferred_element_type=F32).astype(I32)
    pair = (iota(I32, (1, HD), 1) % (HD // 2)).astype(F32)
    frequency = jnp.exp(-(2.0 * pair / HD) * math.log(500000.0))
    angles = (lens + (iota(I32, (otile, 1), 0) // own).astype(F32)) * frequency
    cosine = jnp.cos(angles)
    sine = jnp.sin(angles)
    sine = jnp.where(iota(I32, (otile, HD), 1) < HD // 2, -sine, sine)
    row_of = iota(I32, (tr, per * cache), 0) % n0 // steps
    col_at = iota(I32, (tr, per * cache), 1)
    same_row = row_of == col_at // cache
    col_p = col_at % cache
    line2 = iota(I32, (tr, n0), 0) % n0
    col2 = iota(I32, (tr, n0), 1)
    same_new = (line2 // steps == col2 // steps) & (col2 % steps <= line2 % steps)

    order = [n_t // 2] + [d for d in range(1, n_t) if d != n_t // 2] + [0]

    def query_tile(to, lines):
        return jnp.concatenate([qp[to, lines, h * HD:(h + 1) * HD] for h in range(hpt)], axis=0)

    def over_cache(d):
        to = lax.rem(t + d, n_t)
        kl = pl.ds(pl.multiple_of(to * hpt // GROUP * HD, HD), HD)
        for b in range(own // per):
            keys = k_ref[pl.ds(b * per, per), :, kl].reshape(per * cache, HD)
            vals = v_ref[pl.ds(b * per, per), :, kl].reshape(per * cache, HD)
            sc = lax.dot_general(
                query_tile(to, pl.ds(b * n0, n0)), keys, (((1,), (1,)), ((), ())),
                preferred_element_type=F32) * scale
            limit = jnp.concatenate([lens_rs[b * n0:(b + 1) * n0, :1]] * hpt, axis=0)
            sc = jnp.where(same_row & (col_p < limit), sc, -1e30)
            top = jnp.max(sc, axis=1, keepdims=True)
            e = jnp.exp(sc - top)
            at = d * (own // per) + b
            mc[at] = jnp.broadcast_to(top, (tr, HD))
            lc[at] = jnp.broadcast_to(jnp.sum(e, axis=1, keepdims=True), (tr, HD))
            oc[at] = jnp.dot(e.astype(BF16), vals, preferred_element_type=F32)

    def shrink_part(a, lo, size):
        got = jnp.dot(
            x_ref[:, :, pl.ds(lo, size)].reshape(tile, size), down[a, pl.ds(lo, size)],
            preferred_element_type=F32)
        return jnp.where(idx == a, got, 0.0).reshape(steps, rows, rank)

    shr[...] = shrink_part(z, 0, depth)

    for k in range(1, n_a):
        if k == max(1, n_a - 2):
            q_cp.wait()
            for d in range(1, n_t):
                q_copy(d).wait()
            for j in range(n_t):
                qp[j] = jnp.dot(
                    perm, q_all[j].reshape(otile, hl), preferred_element_type=F32).astype(BF16)
            k_cp.wait()
            v_cp.wait()

        if k == n_a - 1:
            for d in range(1, n_t):
                b_copy(d).wait()
            mine = pl.ds(pl.multiple_of(t * own, own), own)
            total = part[:, mine]
            for d in range(1, n_t):
                total = total + base_in[d - 1]
            base_in[0] = total

        for direction in range(2):
            @pl.when(held(direction, k))
            def _(direction=direction, k=k):
                arrived_uz(direction, k)
                a = z - k if direction == 0 else z + k
                for d in range(1, n_t):
                    u_copy(a, 2 * k - 1 + direction, d).start()

            @pl.when(sends(direction, k))
            def _(direction=direction, k=k):
                uz_copy(direction, k).start()
        for c in range(chunks):
            for direction in range(2):
                @pl.when(arrives(direction, k, c))
                def _(direction=direction, k=k, c=c):
                    arrived_a(direction, k, c)

                @pl.when(a_sends(direction, k, c))
                def _(direction=direction, k=k, c=c):
                    a_copy(direction, k, c).start()

            for direction in range(2):
                @pl.when(arrives(direction, k, c))
                def _(direction=direction, k=k, c=c):
                    a = z - k if direction == 0 else z + k
                    shr[...] += shrink_part(a, c * cd, cd)

            if k == max(1, n_a - 2):
                for d in (order[c // 2::chunks // 2] if c % 2 else []):
                    over_cache(d)
                if gc and c == gc:
                    @pl.when(is_host)
                    def _():
                        gi_copy().wait_recv()
                        gx_copy().wait_recv()
                        skip = end_of
                        names = jnp.concatenate([gidx[...]] * steps, axis=0)
                        total = jnp.zeros((tile, rank), F32)
                        for i in range(n_a - 1):
                            a = lax.rem(skip + 1 + i, n_a)
                            got = jnp.dot(
                                gx[...].reshape(tile, gs), down[a, pl.ds(0, gs)],
                                preferred_element_type=F32)
                            total = total + jnp.where(names == a, got, 0.0)
                        gshr[...] = total.reshape(steps, rows, rank)
                        gr_copy().start()

    if gc:
        @pl.when(is_end)
        def _():
            gr_copy().wait_recv()
            shr[...] += gshr_in[...]

    for d in range(1, n_t):
        s_copy(d).start()
    for d in range(1, n_t):
        u_copy(z, 0, d).wait()
    for k in range(1, n_a):
        for direction in range(2):
            @pl.when(held(direction, k))
            def _(direction=direction, k=k):
                a = z - k if direction == 0 else z + k
                for d in range(1, n_t):
                    u_copy(a, 2 * k - 1 + direction, d).wait()
    for d in range(1, n_t):
        s_copy(d).wait()
    mine = pl.ds(pl.multiple_of(t * own, own), own)
    total = shr[:, mine]
    for d in range(1, n_t):
        total = total + shr_in[d - 1]
    shrunk = total.reshape(otile, rank)
    both = jnp.concatenate([shrunk, shrunk], axis=0)
    line = iota(I32, (2 * otile, rank), 0)
    lane = iota(I32, (2 * otile, rank), 1)
    both = jnp.where((line < otile) == (lane < rank // 2), both, 0.0)
    idx_own = idxs[mine]
    idx_both = jnp.concatenate([idx_own] * (2 * steps), axis=0)
    delta = jnp.zeros((2 * otile, KEY_VALUE_WIDTH), F32)
    for a in range(n_a):
        delta = delta + jnp.dot(
            jnp.where(idx_both == a, both, 0.0).astype(BF16),
            up[a].reshape(rank, KEY_VALUE_WIDTH), preferred_element_type=F32)
    delta = delta.astype(BF16).astype(F32)
    fresh = base_in[0].reshape(otile, width)
    pieces = []
    for h in range(KV):
        one = fresh[:, h * HD:(h + 1) * HD] + delta[:otile, h * HD:(h + 1) * HD]
        pieces.append(one * cosine + pltpu.roll(one, HD // 2, 1) * sine)
    pieces.append(fresh[:, KEY_VALUE_WIDTH:] + delta[otile:])
    new_kv = jnp.concatenate(pieces, axis=1).astype(BF16)
    new_ref[...] = new_kv.reshape(steps, own, width)
    newp[...] = jnp.dot(perm, new_kv, preferred_element_type=F32).astype(BF16)

    def c_copy(d):
        to = lax.rem(t + d, n_t)
        return pltpu.make_async_remote_copy(
            src_ref=ctxs.at[d], dst_ref=ctx_hbm.at[:, pl.ds(pl.multiple_of(t * own, own), own)],
            send_sem=c_send.at[d - 1], recv_sem=c_recv.at[d - 1], device_id={"tensor": to}, device_id_type=MESH)

    for d in order:
        to = lax.rem(t + d, n_t)
        g = to * hpt // GROUP
        kl = pl.ds(pl.multiple_of(g * HD, HD), HD)
        vl = pl.ds(pl.multiple_of(KEY_VALUE_WIDTH + g * HD, HD), HD)
        tiles = []
        for b in range(own // per):
            lines = pl.ds(b * n0, n0)
            at = d * (own // per) + b
            sc = lax.dot_general(
                query_tile(to, lines), newp[lines, kl], (((1,), (1,)), ((), ())),
                preferred_element_type=F32) * scale
            sc = jnp.where(same_new, sc, -1e30)
            top = jnp.maximum(mc[at], jnp.max(sc, axis=1, keepdims=True))
            e = jnp.exp(sc - top[:, :n0])
            less = jnp.exp(mc[at] - top)
            tot = lc[at] * less + jnp.sum(e, axis=1, keepdims=True)
            o = oc[at] * less + jnp.dot(e.astype(BF16), newp[lines, vl], preferred_element_type=F32)
            o = (o / tot).astype(BF16)
            tiles.append(jnp.concatenate([o[h * n0:(h + 1) * n0] for h in range(hpt)], axis=1))
        ctxp = jnp.concatenate(tiles, axis=0)
        ctxs[d] = lax.dot_general(
            perm, ctxp, (((0,), (0,)), ((), ())), preferred_element_type=F32
        ).astype(BF16).reshape(steps, own, hl)
        if d:
            c_copy(d).start()
    own_cp = pltpu.make_async_copy(ctxs.at[0], ctx_hbm.at[:, mine], loc.at[7])
    own_cp.start()

    for k in range(n_a):
        for direction in range(2):
            @pl.when(sends(direction, k))
            def _(direction=direction, k=k):
                uz_copy(direction, k).wait_send()

            for c in range(chunks):
                @pl.when(a_sends(direction, k, c))
                def _(direction=direction, k=k, c=c):
                    a_copy(direction, k, c).wait_send()

    if gc:
        @pl.when(is_end)
        def _():
            gi_copy().wait_send()
            gx_copy().wait_send()

        @pl.when(is_host)
        def _():
            gr_copy().wait_send()
    own_cp.wait()
    for d in range(1, n_t):
        c_copy(d).wait()


def body(
    normed_layer_inputs, key_value_weight, adapter_down_weight, adapter_up_weight,
    request_adapter_index, queries, stored_cache_keys, stored_cache_values, filled_cache_length,
):
    n_a = lax.axis_size("adapter")
    n_t = lax.axis_size("tensor")
    steps, rows, depth = normed_layer_inputs.shape
    own = rows // n_t
    otile = steps * own
    width = key_value_weight.shape[1]
    rank = adapter_down_weight.shape[2]
    hl = queries.shape[2]
    hpt = hl // HD
    per = 16 // steps
    chunks = 8
    uq = rank // n_t

    vm = pl.BlockSpec(memory_space=pltpu.VMEM)
    hbm = pl.BlockSpec(memory_space=pltpu.HBM)
    dma = pltpu.SemaphoreType.DMA
    context, new_kv = pl.pallas_call(
        functools.partial(kernel, n_a, n_t, chunks),
        out_shape=(
            jax.ShapeDtypeStruct((steps, rows, hl), BF16),
            jax.ShapeDtypeStruct((steps, own, width), BF16),
        ),
        in_specs=[vm] * 2 + [hbm] * 7,
        out_specs=(hbm, vm),
        scratch_shapes=[
            pltpu.VMEM((steps, rows, depth), BF16),
            pltpu.VMEM((depth, width), BF16),
            pltpu.VMEM((n_a, depth, rank), BF16),
            pltpu.VMEM((n_a, n_t, uq, KEY_VALUE_WIDTH), BF16),
            pltpu.VMEM(stored_cache_keys.shape, BF16),
            pltpu.VMEM(stored_cache_values.shape, BF16),
            pltpu.VMEM((n_t, steps, own, hl), BF16),
            pltpu.VMEM((n_t, otile, hl), BF16),
            pltpu.VMEM((steps, rows, width), F32),
            pltpu.VMEM((n_t - 1, steps, own, width), F32),
            pltpu.VMEM((steps, rows, rank), F32),
            pltpu.VMEM((n_t - 1, steps, own, rank), F32),
            pltpu.VMEM((otile, width), BF16),
            pltpu.VMEM((n_t, steps, own, hl), BF16),
            *[pltpu.VMEM((n_t * (own // per), hpt * per * steps, HD), F32)] * 3,
            pltpu.VMEM((rows, rank), jnp.int32),
            pltpu.VMEM((steps, rows, max(128, 3 * depth // 8)), BF16),
            pltpu.VMEM((rows, rank), jnp.int32),
            *[pltpu.VMEM((steps, rows, rank), F32)] * 2,
            dma((6,)),
            dma((8,)),
            dma((2, n_a, chunks)), dma((2, n_a, chunks)),
            dma((2 * n_a, n_t - 1)), dma((2 * n_a, n_t - 1)),
            dma((2, n_a)), dma((2, n_a)),
            dma((n_t - 1,)), dma((n_t - 1,)),
            dma((n_t - 1,)), dma((n_t - 1,)),
            dma((n_t - 1,)), dma((n_t - 1,)),
            dma((n_t - 1,)), dma((n_t - 1,)),
        ],
        compiler_params=pltpu.CompilerParams(
            collective_id=0, has_side_effects=True, vmem_limit_bytes=63 * 1024 * 1024),
    )(
        request_adapter_index.reshape(1, rows), filled_cache_length.reshape(1, own),
        normed_layer_inputs, key_value_weight, adapter_down_weight,
        adapter_up_weight.reshape(n_t, uq, KEY_VALUE_WIDTH), queries,
        stored_cache_keys, stored_cache_values,
    )
    return (context, new_kv)


def solution(mesh):
    in_specs = (
        P(None, ("groups", "adapter"), "tensor"),
        P("tensor", None),
        P(("groups", "adapter"), "tensor", None),
        P(("groups", "adapter"), None, None, None),
        P(("groups", "adapter"), None),
        P(None, ("groups", "adapter"), "tensor"),
        P(("groups", "adapter", "tensor"), None, None),
        P(("groups", "adapter", "tensor"), None, None),
        P(("groups", "adapter", "tensor")),
    )
    out_specs = (
        P(None, ("groups", "adapter"), "tensor"),
        P(None, ("groups", "adapter", "tensor"), None),
    )
    return jax.shard_map(body, mesh=mesh, in_specs=in_specs, out_specs=out_specs, check_vma=False)
```

```python
import functools
import math

import jax
import jax.numpy as jnp
from jax import lax
from jax.experimental import pallas as pl
from jax.experimental.pallas import tpu as pltpu
from jax.sharding import PartitionSpec as P

HQ = 32
KV = 4
HD = 128
KEY_VALUE_WIDTH = 512
GROUP = HQ // KV
MESH = pl.DeviceIdType.MESH
F32 = jnp.float32
BF16 = jnp.bfloat16


def kernel(
    n_a, n_t, chunks,
    idx_ref, len_ref,
    x_hbm, w_hbm, a_hbm, u_hbm, q_hbm, k_hbm, v_hbm,
    ctx_hbm, new_ref,
    x_ref, w_ref, down, up, k_ref, v_ref, q_all, qp,
    part, base_in, shr, shr_in, newp, ctxs, oc, mc, lc, idxs, gx, gidx, gshr, gshr_in,
    guest, loc, a_send, a_recv, u_send, u_recv, uz_send, uz_recv,
    q_send, q_recv, b_send, b_recv, s_send, s_recv, c_send, c_recv,
):
    z = lax.axis_index("adapter")
    t = lax.axis_index("tensor")
    steps, rows, depth = x_ref.shape
    own = rows // n_t
    width = w_ref.shape[1]
    tile = steps * rows
    otile = steps * own
    cd = depth // chunks
    uq = up.shape[2]
    hl = q_hbm.shape[2]
    hpt = hl // HD

    cache = k_ref.shape[1]
    per = 16 // steps
    n0 = per * steps
    tr = n0 * hpt
    iota = lax.broadcasted_iota
    I32 = jnp.int32
    scale = 1.0 / math.sqrt(HD)

    def column(row):
        n = row.shape[1]
        eye = iota(I32, (n, n), 0) == iota(I32, (n, n), 1)
        return jnp.sum(jnp.where(eye, row.astype(F32), 0.0), axis=1, keepdims=True)

    x_cp = pltpu.make_async_copy(x_hbm, x_ref, loc.at[0])
    w_cp = pltpu.make_async_copy(w_hbm, w_ref, loc.at[1])
    a_cp = pltpu.make_async_copy(a_hbm.at[0], down.at[z], loc.at[2])
    u_cp = pltpu.make_async_copy(u_hbm.at[t], up.at[z, t], loc.at[3])
    q_cp = pltpu.make_async_copy(
        q_hbm.at[:, pl.ds(pl.multiple_of(t * own, own), own)], q_all.at[t], loc.at[4])
    k_cp = pltpu.make_async_copy(k_hbm, k_ref, loc.at[5])
    v_cp = pltpu.make_async_copy(v_hbm, v_ref, loc.at[6])
    for cp in (a_cp, u_cp, x_cp, w_cp, q_cp, k_cp, v_cp):
        cp.start()

    rank = down.shape[2]
    idxs[...] = jnp.broadcast_to(column(idx_ref[...]).astype(I32), (rows, rank))

    gc = 3 if n_a >= 4 else 0
    gs = gc * cd
    is_end = jnp.logical_or(z == 0, z == n_a - 1)
    is_host = jnp.logical_or(z == 1, z == n_a - 2)
    host_of = jnp.where(z == 0, 1, n_a - 2)
    end_of = jnp.where(z == 1, 0, n_a - 1)

    def guest_copy(i, src, dst, to):
        return pltpu.make_async_remote_copy(
            src_ref=src, dst_ref=dst, send_sem=guest.at[2 * i], recv_sem=guest.at[2 * i + 1],
            device_id={"adapter": to}, device_id_type=MESH)

    def gx_copy():
        return guest_copy(0, x_hbm.at[:, :, pl.ds(0, gs)], gx, host_of)

    def gi_copy():
        return guest_copy(1, idxs, gidx, host_of)

    def gr_copy():
        return guest_copy(2, gshr, gshr_in, end_of)

    barrier = pltpu.get_barrier_semaphore()
    for d in range(1, n_t):
        pl.semaphore_signal(barrier, inc=1, device_id={"tensor": lax.rem(t + d, n_t)}, device_id_type=MESH)

    @pl.when(z > 0)
    def _():
        pl.semaphore_signal(barrier, inc=1, device_id={"adapter": z - 1}, device_id_type=MESH)

    @pl.when(z < n_a - 1)
    def _():
        pl.semaphore_signal(barrier, inc=1, device_id={"adapter": z + 1}, device_id_type=MESH)

    pl.semaphore_wait(barrier, n_t - 1 + jnp.where(z > 0, 1, 0) + jnp.where(z < n_a - 1, 1, 0))

    def a_copy(direction, k, c):
        a = z - k if direction == 0 else z + k
        to = z + 1 if direction == 0 else z - 1
        block = down.at[a, pl.ds(c * cd, cd)]
        return pltpu.make_async_remote_copy(
            src_ref=block, dst_ref=block, send_sem=a_send.at[direction, k, c],
            recv_sem=a_recv.at[direction, k, c], device_id={"adapter": to}, device_id_type=MESH)

    def uz_copy(direction, k):
        a = z - k if direction == 0 else z + k
        to = z + 1 if direction == 0 else z - 1
        block = up.at[a, t]
        return pltpu.make_async_remote_copy(
            src_ref=block, dst_ref=block, send_sem=uz_send.at[direction, k],
            recv_sem=uz_recv.at[direction, k], device_id={"adapter": to}, device_id_type=MESH)

    def held(direction, k):
        return z >= k if direction == 0 else z + k < n_a

    def sends(direction, k):
        return jnp.logical_and(held(direction, k), z < n_a - 1 if direction == 0 else z > 0)

    def arrives(direction, k, c):
        if c >= gc:
            return held(direction, k)
        return jnp.logical_and(held(direction, k), z < n_a - 1 if direction == 0 else z > 0)

    def a_sends(direction, k, c):
        if c >= gc:
            return sends(direction, k)
        return jnp.logical_and(held(direction, k), z < n_a - 2 if direction == 0 else z > 1)

    def u_copy(a, slot, d):
        block = up.at[a, t]
        return pltpu.make_async_remote_copy(
            src_ref=block, dst_ref=block, send_sem=u_send.at[slot, d - 1],
            recv_sem=u_recv.at[slot, d - 1], device_id={"tensor": lax.rem(t + d, n_t)}, device_id_type=MESH)

    def arrived_a(direction, k, c):
        a = z - k if direction == 0 else z + k
        block = down.at[a, pl.ds(c * cd, cd)]
        pltpu.make_async_copy(block, block, a_recv.at[direction, k - 1, c]).wait()

    def arrived_uz(direction, k):
        a = z - k if direction == 0 else z + k
        block = up.at[a, t]
        pltpu.make_async_copy(block, block, uz_recv.at[direction, k - 1]).wait()

    u_cp.wait()
    for direction in range(2):
        @pl.when(sends(direction, 0))
        def _(direction=direction):
            uz_copy(direction, 0).start()
    a_cp.wait()
    for c in range(chunks):
        for direction in range(2):
            @pl.when(a_sends(direction, 0, c))
            def _(direction=direction, c=c):
                a_copy(direction, 0, c).start()

        if gc and c == chunks // 2 - 1:
            @pl.when(is_end)
            def _():
                gi_copy().start()
                gx_copy().start()

    def q_copy(d):
        to = lax.rem(t + d, n_t)
        return pltpu.make_async_remote_copy(
            src_ref=q_hbm.at[:, pl.ds(pl.multiple_of(to * own, own), own)], dst_ref=q_all.at[t],
            send_sem=q_send.at[d - 1], recv_sem=q_recv.at[d - 1], device_id={"tensor": to}, device_id_type=MESH)

    def b_copy(d):
        to = lax.rem(t + d, n_t)
        return pltpu.make_async_remote_copy(
            src_ref=part.at[:, pl.ds(pl.multiple_of(to * own, own), own)], dst_ref=base_in.at[d - 1],
            send_sem=b_send.at[d - 1], recv_sem=b_recv.at[d - 1], device_id={"tensor": to}, device_id_type=MESH)

    def s_copy(d):
        to = lax.rem(t + d, n_t)
        return pltpu.make_async_remote_copy(
            src_ref=shr.at[:, pl.ds(pl.multiple_of(to * own, own), own)], dst_ref=shr_in.at[d - 1],
            send_sem=s_send.at[d - 1], recv_sem=s_recv.at[d - 1], device_id={"tensor": to}, device_id_type=MESH)

    for d in range(1, n_t):
        u_copy(z, 0, d).start()
        q_copy(d).start()

    x_cp.wait()
    w_cp.wait()
    bn = 256

    def base_step(i, carry):
        cols = pl.ds(pl.multiple_of(i * bn, bn), bn)
        part[:, :, cols] = jnp.dot(
            x_ref[...].reshape(tile, depth), w_ref[:, cols], preferred_element_type=F32
        ).reshape(steps, rows, bn)
        return carry

    lax.fori_loop(0, width // bn, base_step, 0)
    for d in range(1, n_t):
        b_copy(d).start()

    idx = jnp.concatenate([idxs[...]] * steps, axis=0)
    i0 = iota(I32, (otile, otile), 0)
    perm = jnp.where(
        iota(I32, (otile, otile), 1) == (i0 % steps) * own + i0 // steps, 1.0, 0.0).astype(BF16)
    lens = jnp.concatenate([column(len_ref[...])] * steps, axis=0)
    lens_rs = jnp.dot(
        perm, jnp.broadcast_to(lens, (otile, HD)).astype(BF16), preferred_element_type=F32).astype(I32)
    pair = (iota(I32, (1, HD), 1) % (HD // 2)).astype(F32)
    frequency = jnp.exp(-(2.0 * pair / HD) * math.log(500000.0))
    angles = (lens + (iota(I32, (otile, 1), 0) // own).astype(F32)) * frequency
    cosine = jnp.cos(angles)
    sine = jnp.sin(angles)
    sine = jnp.where(iota(I32, (otile, HD), 1) < HD // 2, -sine, sine)
    row_of = iota(I32, (tr, per * cache), 0) % n0 // steps
    col_at = iota(I32, (tr, per * cache), 1)
    same_row = row_of == col_at // cache
    col_p = col_at % cache
    line2 = iota(I32, (tr, n0), 0) % n0
    col2 = iota(I32, (tr, n0), 1)
    same_new = (line2 // steps == col2 // steps) & (col2 % steps <= line2 % steps)

    order = [n_t // 2] + [d for d in range(1, n_t) if d != n_t // 2] + [0]

    def query_tile(to, lines):
        return jnp.concatenate([qp[to, lines, h * HD:(h + 1) * HD] for h in range(hpt)], axis=0)

    def over_cache(d):
        to = lax.rem(t + d, n_t)
        kl = pl.ds(pl.multiple_of(to * hpt // GROUP * HD, HD), HD)
        for b in range(own // per):
            keys = k_ref[pl.ds(b * per, per), :, kl].reshape(per * cache, HD)
            vals = v_ref[pl.ds(b * per, per), :, kl].reshape(per * cache, HD)
            sc = lax.dot_general(
                query_tile(to, pl.ds(b * n0, n0)), keys, (((1,), (1,)), ((), ())),
                preferred_element_type=F32) * scale
            limit = jnp.concatenate([lens_rs[b * n0:(b + 1) * n0, :1]] * hpt, axis=0)
            sc = jnp.where(same_row & (col_p < limit), sc, -1e30)
            top = jnp.max(sc, axis=1, keepdims=True)
            e = jnp.exp(sc - top)
            at = d * (own // per) + b
            mc[at] = jnp.broadcast_to(top, (tr, HD))
            lc[at] = jnp.broadcast_to(jnp.sum(e, axis=1, keepdims=True), (tr, HD))
            oc[at] = jnp.dot(e.astype(BF16), vals, preferred_element_type=F32)

    def shrink_part(a, lo, size):
        got = jnp.dot(
            x_ref[:, :, pl.ds(lo, size)].reshape(tile, size), down[a, pl.ds(lo, size)],
            preferred_element_type=F32)
        return jnp.where(idx == a, got, 0.0).reshape(steps, rows, rank)

    shr[...] = shrink_part(z, 0, depth)

    for k in range(1, n_a):
        if k == max(1, n_a - 2):
            q_cp.wait()
            for d in range(1, n_t):
                q_copy(d).wait()
            for j in range(n_t):
                qp[j] = jnp.dot(
                    perm, q_all[j].reshape(otile, hl), preferred_element_type=F32).astype(BF16)
            k_cp.wait()
            v_cp.wait()

        if k == n_a - 1:
            for d in range(1, n_t):
                b_copy(d).wait()
            mine = pl.ds(pl.multiple_of(t * own, own), own)
            total = part[:, mine]
            for d in range(1, n_t):
                total = total + base_in[d - 1]
            base_in[0] = total

        for direction in range(2):
            @pl.when(held(direction, k))
            def _(direction=direction, k=k):
                arrived_uz(direction, k)
                a = z - k if direction == 0 else z + k
                for d in range(1, n_t):
                    u_copy(a, 2 * k - 1 + direction, d).start()

            @pl.when(sends(direction, k))
            def _(direction=direction, k=k):
                uz_copy(direction, k).start()
        for c in range(chunks):
            for direction in range(2):
                @pl.when(arrives(direction, k, c))
                def _(direction=direction, k=k, c=c):
                    arrived_a(direction, k, c)

                @pl.when(a_sends(direction, k, c))
                def _(direction=direction, k=k, c=c):
                    a_copy(direction, k, c).start()

            for direction in range(2):
                @pl.when(arrives(direction, k, c))
                def _(direction=direction, k=k, c=c):
                    a = z - k if direction == 0 else z + k
                    shr[...] += shrink_part(a, c * cd, cd)

            if k == n_a - 1:
                for d in (order[c // 2::chunks // 2] if c % 2 == 0 else []):
                    over_cache(d)
            if k == n_a - 2:
                if gc and c == chunks - 1:
                    @pl.when(is_host)
                    def _():
                        gi_copy().wait_recv()
                        gx_copy().wait_recv()
                        skip = end_of
                        names = jnp.concatenate([gidx[...]] * steps, axis=0)
                        total = jnp.zeros((tile, rank), F32)
                        for i in range(n_a - 1):
                            a = lax.rem(skip + 1 + i, n_a)
                            got = jnp.dot(
                                gx[...].reshape(tile, gs), down[a, pl.ds(0, gs)],
                                preferred_element_type=F32)
                            total = total + jnp.where(names == a, got, 0.0)
                        gshr[...] = total.reshape(steps, rows, rank)
                        gr_copy().start()

    if gc:
        @pl.when(is_end)
        def _():
            gr_copy().wait_recv()
            shr[...] += gshr_in[...]

    for d in range(1, n_t):
        s_copy(d).start()
    for d in range(1, n_t):
        u_copy(z, 0, d).wait()
    for k in range(1, n_a):
        for direction in range(2):
            @pl.when(held(direction, k))
            def _(direction=direction, k=k):
                a = z - k if direction == 0 else z + k
                for d in range(1, n_t):
                    u_copy(a, 2 * k - 1 + direction, d).wait()
    for d in range(1, n_t):
        s_copy(d).wait()
    mine = pl.ds(pl.multiple_of(t * own, own), own)
    total = shr[:, mine]
    for d in range(1, n_t):
        total = total + shr_in[d - 1]
    shrunk = total.reshape(otile, rank)
    both = jnp.concatenate([shrunk, shrunk], axis=0)
    line = iota(I32, (2 * otile, rank), 0)
    lane = iota(I32, (2 * otile, rank), 1)
    both = jnp.where((line < otile) == (lane < rank // 2), both, 0.0)
    idx_own = idxs[mine]
    idx_both = jnp.concatenate([idx_own] * (2 * steps), axis=0)
    delta = jnp.zeros((2 * otile, KEY_VALUE_WIDTH), F32)
    for a in range(n_a):
        delta = delta + jnp.dot(
            jnp.where(idx_both == a, both, 0.0).astype(BF16),
            up[a].reshape(rank, KEY_VALUE_WIDTH), preferred_element_type=F32)
    delta = delta.astype(BF16).astype(F32)
    fresh = base_in[0].reshape(otile, width)
    pieces = []
    for h in range(KV):
        one = fresh[:, h * HD:(h + 1) * HD] + delta[:otile, h * HD:(h + 1) * HD]
        pieces.append(one * cosine + pltpu.roll(one, HD // 2, 1) * sine)
    pieces.append(fresh[:, KEY_VALUE_WIDTH:] + delta[otile:])
    new_kv = jnp.concatenate(pieces, axis=1).astype(BF16)
    new_ref[...] = new_kv.reshape(steps, own, width)
    newp[...] = jnp.dot(perm, new_kv, preferred_element_type=F32).astype(BF16)

    def c_copy(d):
        to = lax.rem(t + d, n_t)
        return pltpu.make_async_remote_copy(
            src_ref=ctxs.at[d], dst_ref=ctx_hbm.at[:, pl.ds(pl.multiple_of(t * own, own), own)],
            send_sem=c_send.at[d - 1], recv_sem=c_recv.at[d - 1], device_id={"tensor": to}, device_id_type=MESH)

    for d in order:
        to = lax.rem(t + d, n_t)
        g = to * hpt // GROUP
        kl = pl.ds(pl.multiple_of(g * HD, HD), HD)
        vl = pl.ds(pl.multiple_of(KEY_VALUE_WIDTH + g * HD, HD), HD)
        tiles = []
        for b in range(own // per):
            lines = pl.ds(b * n0, n0)
            at = d * (own // per) + b
            sc = lax.dot_general(
                query_tile(to, lines), newp[lines, kl], (((1,), (1,)), ((), ())),
                preferred_element_type=F32) * scale
            sc = jnp.where(same_new, sc, -1e30)
            top = jnp.maximum(mc[at], jnp.max(sc, axis=1, keepdims=True))
            e = jnp.exp(sc - top[:, :n0])
            less = jnp.exp(mc[at] - top)
            tot = lc[at] * less + jnp.sum(e, axis=1, keepdims=True)
            o = oc[at] * less + jnp.dot(e.astype(BF16), newp[lines, vl], preferred_element_type=F32)
            o = (o / tot).astype(BF16)
            tiles.append(jnp.concatenate([o[h * n0:(h + 1) * n0] for h in range(hpt)], axis=1))
        ctxp = jnp.concatenate(tiles, axis=0)
        ctxs[d] = lax.dot_general(
            perm, ctxp, (((0,), (0,)), ((), ())), preferred_element_type=F32
        ).astype(BF16).reshape(steps, own, hl)
        if d:
            c_copy(d).start()
    own_cp = pltpu.make_async_copy(ctxs.at[0], ctx_hbm.at[:, mine], loc.at[7])
    own_cp.start()

    for k in range(n_a):
        for direction in range(2):
            @pl.when(sends(direction, k))
            def _(direction=direction, k=k):
                uz_copy(direction, k).wait_send()

            for c in range(chunks):
                @pl.when(a_sends(direction, k, c))
                def _(direction=direction, k=k, c=c):
                    a_copy(direction, k, c).wait_send()

    if gc:
        @pl.when(is_end)
        def _():
            gi_copy().wait_send()
            gx_copy().wait_send()

        @pl.when(is_host)
        def _():
            gr_copy().wait_send()
    own_cp.wait()
    for d in range(1, n_t):
        c_copy(d).wait()


def hand_over(steps, ctx_in, new_in, ctx_out, new_out, sems):
    copies = []
    for i in range(steps):
        copies.append(pltpu.make_async_copy(ctx_in.at[i], ctx_out.at[i], sems.at[2 * i]))
        copies.append(pltpu.make_async_copy(new_in.at[i], new_out.at[i], sems.at[2 * i + 1]))
    for cp in copies:
        cp.start()
    for cp in copies:
        cp.wait()


def body(
    normed_layer_inputs, key_value_weight, adapter_down_weight, adapter_up_weight,
    request_adapter_index, queries, stored_cache_keys, stored_cache_values, filled_cache_length,
):
    n_a = lax.axis_size("adapter")
    n_t = lax.axis_size("tensor")
    steps, rows, depth = normed_layer_inputs.shape
    own = rows // n_t
    otile = steps * own
    width = key_value_weight.shape[1]
    rank = adapter_down_weight.shape[2]
    hl = queries.shape[2]
    hpt = hl // HD
    per = 16 // steps
    chunks = 8
    uq = rank // n_t

    vm = pl.BlockSpec(memory_space=pltpu.VMEM)
    hbm = pl.BlockSpec(memory_space=pltpu.HBM)
    dma = pltpu.SemaphoreType.DMA
    context, new_kv = pl.pallas_call(
        functools.partial(kernel, n_a, n_t, chunks),
        out_shape=(
            jax.ShapeDtypeStruct((steps, rows, hl), BF16),
            jax.ShapeDtypeStruct((steps, own, width), BF16),
        ),
        in_specs=[vm] * 2 + [hbm] * 7,
        out_specs=(hbm, vm),
        scratch_shapes=[
            pltpu.VMEM((steps, rows, depth), BF16),
            pltpu.VMEM((depth, width), BF16),
            pltpu.VMEM((n_a, depth, rank), BF16),
            pltpu.VMEM((n_a, n_t, uq, KEY_VALUE_WIDTH), BF16),
            pltpu.VMEM(stored_cache_keys.shape, BF16),
            pltpu.VMEM(stored_cache_values.shape, BF16),
            pltpu.VMEM((n_t, steps, own, hl), BF16),
            pltpu.VMEM((n_t, otile, hl), BF16),
            pltpu.VMEM((steps, rows, width), F32),
            pltpu.VMEM((n_t - 1, steps, own, width), F32),
            pltpu.VMEM((steps, rows, rank), F32),
            pltpu.VMEM((n_t - 1, steps, own, rank), F32),
            pltpu.VMEM((otile, width), BF16),
            pltpu.VMEM((n_t, steps, own, hl), BF16),
            *[pltpu.VMEM((n_t * (own // per), hpt * per * steps, HD), F32)] * 3,
            pltpu.VMEM((rows, rank), jnp.int32),
            pltpu.VMEM((steps, rows, max(128, 3 * depth // 8)), BF16),
            pltpu.VMEM((rows, rank), jnp.int32),
            *[pltpu.VMEM((steps, rows, rank), F32)] * 2,
            dma((6,)),
            dma((8,)),
            dma((2, n_a, chunks)), dma((2, n_a, chunks)),
            dma((2 * n_a, n_t - 1)), dma((2 * n_a, n_t - 1)),
            dma((2, n_a)), dma((2, n_a)),
            dma((n_t - 1,)), dma((n_t - 1,)),
            dma((n_t - 1,)), dma((n_t - 1,)),
            dma((n_t - 1,)), dma((n_t - 1,)),
            dma((n_t - 1,)), dma((n_t - 1,)),
        ],
        compiler_params=pltpu.CompilerParams(
            collective_id=0, has_side_effects=True, vmem_limit_bytes=63 * 1024 * 1024),
    )(
        request_adapter_index.reshape(1, rows), filled_cache_length.reshape(1, own),
        normed_layer_inputs, key_value_weight, adapter_down_weight,
        adapter_up_weight.reshape(n_t, uq, KEY_VALUE_WIDTH), queries,
        stored_cache_keys, stored_cache_values,
    )
    pieces = 2 * steps
    return pl.pallas_call(
        functools.partial(hand_over, steps),
        out_shape=(
            jax.ShapeDtypeStruct(context.shape, BF16), jax.ShapeDtypeStruct(new_kv.shape, BF16)),
        in_specs=[hbm] * 2,
        out_specs=(hbm, hbm),
        scratch_shapes=[dma((pieces,))],
    )(context, new_kv)


def solution(mesh):
    in_specs = (
        P(None, ("groups", "adapter"), "tensor"),
        P("tensor", None),
        P(("groups", "adapter"), "tensor", None),
        P(("groups", "adapter"), None, None, None),
        P(("groups", "adapter"), None),
        P(None, ("groups", "adapter"), "tensor"),
        P(("groups", "adapter", "tensor"), None, None),
        P(("groups", "adapter", "tensor"), None, None),
        P(("groups", "adapter", "tensor")),
    )
    out_specs = (
        P(None, ("groups", "adapter"), "tensor"),
        P(None, ("groups", "adapter", "tensor"), None),
    )
    return jax.shard_map(body, mesh=mesh, in_specs=in_specs, out_specs=out_specs, check_vma=False)
```
